1024 devices in a mesh: seq: 64 (over y, z), dp: 16 (over x, core).
Axes of the slice: x: 8, y: 8, z: 8, core: 2. Of those that a mesh axis runs over, the one named last changes fastest.
Arguments:
- queries: bfloat16 [8192, 8192], P('seq', 'dp'), may hold values from -6 to 6
- keys: bfloat16 [8192, 8192], P('seq', 'dp'), may hold values from -0.59765625 to 0.59765625
- values: bfloat16 [8192, 8192], P('seq', 'dp'), may hold values from -6 to 6
- output_gradient: bfloat16 [8192, 8192], P('seq', 'dp'), may hold values from -6 to 6
- log_decay: float32 [64, 8192], P('dp', 'seq'), may hold values from -1 to 0, as said below
- gain: float32 [8192], P('dp'), may hold values from 0.1 to 1.9
Outputs:
- query_grad: bfloat16 [8192, 8192], P('seq', 'dp')
- key_grad: bfloat16 [8192, 8192], P('seq', 'dp')
- value_grad: bfloat16 [8192, 8192], P('seq', 'dp')
- gain_grad: float32 [8192], P('dp')
The draws below stay inside these ranges and needn't reach their ends.
Inputs may be any that keep to these rules, and one draw needn't show every extreme that they name: `log_decay`: negative at every token and head.
All inputs are finite; a program needn't handle non-finite values.
Results may differ from the reference program's by a relative error of at most 0.005.
Values sent between devices are 32-bit elements; how exact they have to be, the bound alone decides.
A program may use at most 128 MiB of HBM per device.

```python
import math
import jax
import jax.numpy as jnp
from jax import lax

H = 64
DH = 128
TOK_DEV = 128
HD = 8192
LENGTH = 8192


def draw_log_decay(key, part):
    keys_all = jax.random.split(key, 7)
    fast_share = 0.4
    picked_items = jax.random.uniform(keys_all[0], (H, 1)) < fast_share
    fast_rate = jnp.exp(jax.random.uniform(keys_all[1], (H, 1), minval=math.log(1.0 / 50.0), maxval=math.log(1.0 / 30.0)))
    slow_rate = jnp.exp(jax.random.uniform(keys_all[2], (H, 1), minval=math.log(0.01 / LENGTH), maxval=math.log(0.1 / LENGTH)))
    base_rate = jnp.where(picked_items, fast_rate, slow_rate)
    block_count = LENGTH // TOK_DEV
    block_factor = jnp.exp(jax.random.uniform(keys_all[3], (H, block_count, 1), minval=-math.log(2.0), maxval=math.log(2.0)))
    block_factor = jnp.broadcast_to(block_factor, (H, block_count, TOK_DEV)).reshape(H, LENGTH)
    token_factor = jax.random.uniform(keys_all[4], (H, LENGTH), minval=0.5, maxval=1.5)
    forgetting_speed = base_rate * block_factor * token_factor
    sequence_indices = jax.random.randint(keys_all[5], (3,), 0, LENGTH)
    objective_numbers = jax.random.uniform(keys_all[6], (3,), minval=0.2, maxval=0.4)
    device_assignment = jnp.arange(LENGTH)
    segment_lengths = jnp.sum(jnp.where(device_assignment[None, :] == sequence_indices[:, None], jnp.log(1.0 - objective_numbers)[:, None], 0.0), axis=0)
    return (-forgetting_speed + segment_lengths[None, :]).astype(jnp.float32)


def block_scale(rng, shape, cuts, smallest, high):
    def one(axis_at, shards_of):
        draws = jax.random.uniform(jax.random.fold_in(jax.random.fold_in(rng, 6), axis_at), (shards_of,), jnp.float32, smallest / len(cuts), high / len(cuts))
        return jnp.repeat(jnp.exp(draws), shape[axis_at] // shards_of).reshape((-1,) + (1,) * (len(shape) - axis_at - 1))

    loudness = one(*cuts[0])
    for cut in cuts[1:]:
        loudness = loudness * one(*cut)
    return loudness


def scatter_about(stream_key, shape, width, bound, cuts=(), kind=jnp.bfloat16):
    drawn = jax.random.normal(stream_key, shape, jnp.float32) * width
    if len(cuts) > 0:
        drawn = block_scale(stream_key, shape, cuts, -0.22, 0.18) * drawn
    return jnp.clip(drawn, min=-bound, max=bound).astype(kind)


def setup_inputs(seed: int = 0) -> dict:
    arg_keys = jax.random.split(jax.random.key(seed), 7)
    return {
        "queries": scatter_about(arg_keys[0], (LENGTH, HD), 1.0, 6.0, ((0, 64), (1, 16))),
        "keys": scatter_about(arg_keys[1], (LENGTH, HD), 0.1, 0.59765625, ((0, 64), (1, 16))),
        "values": scatter_about(arg_keys[2], (LENGTH, HD), 1.0, 6.0, ((0, 64), (1, 16))),
        "output_gradient": scatter_about(arg_keys[3], (LENGTH, HD), 1.0, 6.0, ((0, 64), (1, 16))),
        "log_decay": draw_log_decay(jax.random.fold_in(arg_keys[6], 71), 0),
        "gain": jnp.clip(1.0 + 0.18 * jax.random.normal(arg_keys[5], (HD,), jnp.float32), 0.1, 1.9),
    }


epsilon = 1e-05
highest = lax.Precision.HIGHEST

def block_weights(cum):
    row_index = lax.broadcasted_iota(jnp.int32, (TOK_DEV, TOK_DEV), 0)
    col_index = lax.broadcasted_iota(jnp.int32, (TOK_DEV, TOK_DEV), 1)
    causal_mask = row_index >= col_index
    dispersion_factor = cum[:, :, None] - cum[:, None, :]
    return jnp.where(causal_mask[None], jnp.exp(jnp.minimum(dispersion_factor, 0.0)), 0.0)

def carry_step(state, item):
    decay_now, local_now = item
    return (decay_now[:, None, None] * state + local_now, state)

def reference(queries, keys, values, output_gradient, log_decay, gain):
    blocks = LENGTH // TOK_DEV
    shape_four = (blocks, TOK_DEV, H, DH)
    query_b = queries.reshape(shape_four)
    key_b = keys.reshape(shape_four)
    value_b = values.reshape(shape_four)
    grad_b = output_gradient.reshape(blocks, TOK_DEV, H * DH)
    cumulative = jnp.cumsum(log_decay.reshape(H, blocks, TOK_DEV), axis=2).transpose(1, 0, 2)
    last = cumulative[:, :, -1]
    total_decay = jnp.exp(last)

    def state_of(packed):
        key_now, value_now, cum, lst = packed
        tail_t = jnp.exp(lst[:, None] - cum).T[..., None]
        return jnp.einsum('thd,the->hde', key_now.astype(jnp.float32) * tail_t, value_now.astype(jnp.float32), precision=highest)
    local_state = lax.map(state_of, (key_b, value_b, cumulative, last))
    start_state = jnp.zeros((H, DH, DH), jnp.float32)
    _, incoming = lax.scan(carry_step, start_state, (total_decay, local_state))

    def forward_of(packed):
        query_now, key_now, value_now, grad_now, cum, inc = packed
        query_f = query_now.astype(jnp.float32)
        key_f = key_now.astype(jnp.float32)
        value_f = value_now.astype(jnp.float32)
        weights = block_weights(cum)
        lead_t = jnp.exp(cum).T[..., None]
        similarity_matrix = jnp.einsum('thd,shd->hts', query_f, key_f, precision=highest)
        mixed_b = (similarity_matrix * weights).astype(jnp.bfloat16)
        mixed_f = lax.optimization_barrier(mixed_b).astype(jnp.float32)
        inner = jnp.einsum('hts,shd->thd', mixed_f, value_f, precision=highest)
        outer = jnp.einsum('thd,hde->the', query_f, inc, precision=highest) * lead_t
        attn = (inner + outer).reshape(TOK_DEV, H * DH)
        inv_rms = lax.rsqrt(lax.optimization_barrier(jnp.mean(attn * attn, axis=-1, keepdims=True)) + epsilon)
        normed = attn * inv_rms
        grad_f = grad_now.astype(jnp.float32)
        multiplied_entries = grad_f * gain
        d_attn = (inv_rms * (multiplied_entries - normed * lax.optimization_barrier(jnp.mean(multiplied_entries * normed, axis=-1, keepdims=True)))).astype(jnp.bfloat16)
        gain_part = lax.optimization_barrier(jnp.sum(grad_f * normed, axis=0))
        d_attn_f = lax.optimization_barrier(d_attn).astype(jnp.float32).reshape(TOK_DEV, H, DH)
        local_back = jnp.einsum('thd,the->hde', query_f * lead_t, d_attn_f, precision=highest)
        return (d_attn, gain_part, local_back)
    d_attn_all, gain_parts, local_back = lax.map(forward_of, (query_b, key_b, value_b, grad_b, cumulative, incoming))
    _, later = lax.scan(carry_step, start_state, (total_decay, local_back), reverse=True)

    def grads_of(packed):
        query_now, key_now, value_now, d_now, cum, lst, inc, lat = packed
        query_f = query_now.astype(jnp.float32)
        key_f = key_now.astype(jnp.float32)
        value_f = value_now.astype(jnp.float32)
        d_attn_f = d_now.astype(jnp.float32).reshape(TOK_DEV, H, DH)
        weights = block_weights(cum)
        lead_t = jnp.exp(cum).T[..., None]
        tail_t = jnp.exp(lst[:, None] - cum).T[..., None]
        similarity_matrix = jnp.einsum('thd,shd->hts', query_f, key_f, precision=highest)
        mixed_b = (similarity_matrix * weights).astype(jnp.bfloat16)
        mixed_f = lax.optimization_barrier(mixed_b).astype(jnp.float32)
        dprod = jnp.einsum('thd,shd->hts', d_attn_f, value_f, precision=highest)
        graded_b = (dprod * weights).astype(jnp.bfloat16)
        graded_f = lax.optimization_barrier(graded_b).astype(jnp.float32)
        query_grad = jnp.einsum('hts,shd->thd', graded_f, key_f, precision=highest)
        query_grad = query_grad + jnp.einsum('the,hde->thd', d_attn_f, inc, precision=highest) * lead_t
        key_grad = jnp.einsum('hts,thd->shd', graded_f, query_f, precision=highest)
        key_grad = key_grad + jnp.einsum('the,hde->thd', value_f, lat, precision=highest) * tail_t
        value_grad = jnp.einsum('hts,thd->shd', mixed_f, d_attn_f, precision=highest)
        value_grad = value_grad + jnp.einsum('thd,hde->the', key_f, lat, precision=highest) * tail_t
        return (query_grad.reshape(TOK_DEV, H * DH).astype(jnp.bfloat16), key_grad.reshape(TOK_DEV, H * DH).astype(jnp.bfloat16), value_grad.reshape(TOK_DEV, H * DH).astype(jnp.bfloat16))
    query_grad, key_grad, value_grad = lax.map(grads_of, (query_b, key_b, value_b, d_attn_all, cumulative, last, incoming, later))
    return (query_grad.reshape(LENGTH, H * DH), key_grad.reshape(LENGTH, H * DH), value_grad.reshape(LENGTH, H * DH), lax.optimization_barrier(jnp.sum(gain_parts, axis=0)))
```

```python
import functools

import jax
import jax.numpy as jnp
from jax import lax
from jax.experimental import pallas as pl
from jax.experimental.pallas import tpu as pltpu
from jax.sharding import PartitionSpec as P

MESH = pl.DeviceIdType.MESH
EPS = 1e-05
F32, BF16 = jnp.float32, jnp.bfloat16
HIGHEST = lax.Precision.HIGHEST
H, D, T = 4, 128, 128
SIDE, N_SEQ, N_DP = 8, 64, 16


def _ring(step):
    return min(step, SIDE - step)


STEPS = sorted(
    ((dy, dz) for dy in range(SIDE) for dz in range(SIDE) if dy or dz),
    key=lambda s: -(_ring(s[0]) + _ring(s[1])),
)
DP_STEPS = sorted(range(1, N_DP), key=lambda s: -_ring(s // 2))


def dot(a, b, ca=1, cb=0, precision=None):
    return lax.dot_general(
        a, b, (((ca,), (cb,)), ((), ())), precision=precision, preferred_element_type=F32
    )


def split(x):
    hi = x.astype(BF16)
    return hi, (x - hi.astype(F32)).astype(BF16)


def dot_fine_left(a, b, ca=1, cb=0):
    hi, lo = split(a)
    return dot(hi, b, ca, cb) + dot(lo, b, ca, cb)


def dot_fine_right(a, b, ca=1, cb=0):
    hi, lo = split(b)
    return dot(a, hi, ca, cb) + dot(a, lo, ca, cb)


def kernel(
    q_ref, k_ref, v_ref, g_ref, ld_ref, gain_ref,
    dq_ref, dk_ref, dv_ref, dg_ref,
    snd1, rcv1, out1, inc, snd2, rcv2, out2, lat, dec_snd, dec,
    stat_snd, stat, gz_snd, gz, gy_snd, gy,
    qt, weights, mixed, attn, d_attn, kg, vg,
    send_sems, recv_sems,
):
    me = lax.axis_index("seq")
    mine = lax.axis_index("dp")
    y, z = lax.div(me, SIDE), lax.rem(me, SIDE)
    rows = [lax.rem(y + k, SIDE) * SIDE for k in range(SIDE)]
    cols = [lax.rem(z + k, SIDE) for k in range(SIDE)]
    peers = [rows[dy] + cols[dz] for dy, dz in STEPS]
    partners = [lax.rem(mine + k, N_DP) for k in DP_STEPS]

    barrier = pltpu.get_barrier_semaphore()
    for p in peers:
        pl.semaphore_signal(barrier, inc=1, device_id={"seq": p}, device_id_type=MESH)
    for p in partners:
        pl.semaphore_signal(barrier, inc=1, device_id={"dp": p}, device_id_type=MESH)

    def send(src, dst, at, where):
        pltpu.make_async_remote_copy(
            src_ref=src, dst_ref=dst, send_sem=send_sems.at[at], recv_sem=recv_sems.at[at],
            device_id=where, device_id_type=MESH,
        ).start()

    def arrived(buffer, count, at, sems=recv_sems):
        part = buffer.at[pl.ds(0, count)]
        pltpu.make_async_copy(part, part, sems.at[at]).wait()

    def exchange(src, dst, at):
        for p in peers:
            send(src.at[p], dst.at[me], at, {"seq": p})
        dst[me] = src[me]

    row_i = lax.broadcasted_iota(jnp.int32, (T, T), 0)
    col_i = lax.broadcasted_iota(jnp.int32, (T, T), 1)
    lower = row_i >= col_i
    log_decay = ld_ref[...]
    cum_row = dot(log_decay, jnp.where(row_i <= col_i, 1.0, 0.0), precision=HIGHEST)
    cum_col = dot(jnp.where(lower, 1.0, 0.0), log_decay, 1, 1, precision=HIGHEST)
    last_row = cum_row[:, T - 1:]
    tail_row = jnp.exp(last_row - cum_row)
    lead_row = jnp.exp(cum_row)
    tail_col = jnp.exp(cum_col[T - 1:, :] - cum_col)
    lead_col = jnp.exp(cum_col)
    total = jnp.broadcast_to(jnp.exp(last_row), (H, T))

    def head(ref, h):
        return ref[:, h * D:(h + 1) * D]

    kt = []
    for h in range(H):
        dec_snd[h] = total[h:h + 1, :]
        kt.append(jnp.transpose(head(k_ref, h)))
        weighted = kt[h].astype(F32) * tail_row[h:h + 1, :]
        local = dot_fine_left(weighted, head(v_ref, h))
        snd1[pl.ds(16 * h, 16)] = local.reshape(16, 8, D)

    pl.semaphore_wait(barrier, N_SEQ - 1 + N_DP - 1)
    for p in peers:
        send(dec_snd.at[lax.div(p, 16)], dec.at[me], 1, {"seq": p})
    dec[me] = dec_snd[lax.div(me, 16)]
    exchange(snd1, rcv1, 0)

    for h in range(H):
        qh = head(q_ref, h)
        qt[h] = jnp.transpose(qh)
        w = jnp.where(
            lower,
            jnp.exp(jnp.minimum(cum_col[:, h:h + 1] - cum_row[h:h + 1, :], 0.0)),
            0.0,
        )
        weights[h] = w
        m = (dot(qh, kt[h]) * w).astype(BF16)
        mixed[h] = m
        attn[h] = dot(m, head(v_ref, h))

    arrived(dec, N_SEQ - 1, 1)
    arrived(rcv1, N_SEQ - 1, 0)
    state = jnp.zeros((8, D), F32)
    for c in range(N_SEQ):
        out1[c] = state
        state = dec[c] * state + rcv1[c]
    exchange(out1, inc, 2)
    arrived(inc, N_SEQ - 1, 2)

    def state_of(buffer, h):
        return buffer[pl.ds(16 * h, 16)].reshape(D, D)

    square = jnp.zeros((T, D), F32)
    cross = jnp.zeros((T, D), F32)
    for h in range(H):
        outer = dot_fine_right(head(q_ref, h), state_of(inc, h)) * lead_col[:, h:h + 1]
        a = attn[h] + outer
        attn[h] = a
        scaled = head(g_ref, h).astype(F32) * gain_ref[:, h * D:(h + 1) * D]
        square = square + a * a
        cross = cross + scaled * a
    square = jnp.sum(square, axis=1, keepdims=True)
    cross = jnp.sum(cross, axis=1, keepdims=True)
    both = jnp.where(col_i == 0, square, jnp.where(col_i == 1, cross, 0.0))
    stat_snd[...] = jnp.transpose(both)[0:8, :]
    for p in partners:
        send(stat_snd, stat.at[mine], 3, {"dp": p})
    stat[mine] = stat_snd[...]
    arrived(stat, N_DP - 1, 3)
    sums = stat[0]
    for c in range(1, N_DP):
        sums = sums + stat[c]
    sums = jnp.transpose(jnp.concatenate([sums] * 16, axis=0)) * (1.0 / (N_DP * H * D))
    gz_snd[...] = jnp.zeros_like(gz_snd)
    inv = lax.rsqrt(sums[:, 0:1] + EPS)
    cross_mean = inv * sums[:, 1:2]

    for h in range(H):
        g = head(g_ref, h).astype(F32)
        scaled = g * gain_ref[:, h * D:(h + 1) * D]
        normed = attn[h] * inv
        d = (inv * (scaled - normed * cross_mean)).astype(BF16)
        d_attn[h] = d
        gz_snd[h:h + 1, :] = jnp.sum(g * normed, axis=0, keepdims=True)
        weighted = qt[h].astype(F32) * lead_row[h:h + 1, :]
        snd2[pl.ds(16 * h, 16)] = dot_fine_left(weighted, d).reshape(16, 8, D)
    exchange(snd2, rcv2, 4)
    for k in range(1, SIDE):
        send(gz_snd, gz.at[z], 5, {"seq": rows[0] + cols[k]})
    gz[z] = gz_snd[...]

    for h in range(H):
        qh, kh, vh, d = head(q_ref, h), head(k_ref, h), head(v_ref, h), d_attn[h]
        graded = (dot(d, vh, 1, 1) * weights[h]).astype(BF16)
        far = dot_fine_right(d, state_of(inc, h), 1, 1) * lead_col[:, h:h + 1]
        dq_ref[:, h * D:(h + 1) * D] = (dot(graded, kh) + far).astype(BF16)
        kg[h] = dot(graded, qh, 0, 0)
        vg[h] = dot(mixed[h], d, 0, 0)

    arrived(rcv2, N_SEQ - 1, 4)
    state = jnp.zeros((8, D), F32)
    for c in reversed(range(N_SEQ)):
        out2[c] = state
        state = dec[c] * state + rcv2[c]
    exchange(out2, lat, 6)
    arrived(gz, SIDE - 1, 5)
    part = gz[0]
    for c in range(1, SIDE):
        part = part + gz[c]
    gy_snd[...] = part
    for k in range(1, SIDE):
        send(gy_snd, gy.at[y], 7, {"seq": rows[k] + cols[0]})
    gy[y] = gy_snd[...]

    arrived(lat, N_SEQ - 1, 6)
    for h in range(H):
        kh, vh, tail = head(k_ref, h), head(v_ref, h), tail_col[:, h:h + 1]
        late = state_of(lat, h)
        dk_ref[:, h * D:(h + 1) * D] = (kg[h] + dot_fine_right(vh, late, 1, 1) * tail).astype(BF16)
        dv_ref[:, h * D:(h + 1) * D] = (vg[h] + dot_fine_right(kh, late) * tail).astype(BF16)
    arrived(gy, SIDE - 1, 7)
    part = gy[0]
    for c in range(1, SIDE):
        part = part + gy[c]
    dg_ref[...] = part[0:H, :]

    for buffer, count, at in (
        (rcv1, N_SEQ - 1, 0), (dec, N_SEQ - 1, 1), (inc, N_SEQ - 1, 2), (stat, N_DP - 1, 3),
        (rcv2, N_SEQ - 1, 4), (gz, SIDE - 1, 5), (lat, N_SEQ - 1, 6), (gy, SIDE - 1, 7),
    ):
        arrived(buffer, count, at, send_sems)


def on_device(queries, keys, values, output_gradient, log_decay, gain):
    vmem = pl.BlockSpec(memory_space=pltpu.VMEM)
    wide = jax.ShapeDtypeStruct((T, H * D), BF16)
    tiles = pltpu.VMEM((N_SEQ, 8, D), F32)
    dq, dk, dv, dg = pl.pallas_call(
        kernel,
        out_shape=(wide, wide, wide, jax.ShapeDtypeStruct((H, D), F32)),
        in_specs=[vmem] * 6,
        out_specs=(vmem,) * 4,
        scratch_shapes=[
            tiles, tiles, tiles, tiles, tiles, tiles, tiles, tiles,
            pltpu.VMEM((H, 1, D), F32),
            pltpu.VMEM((N_SEQ, 1, D), F32),
            pltpu.VMEM((8, T), F32),
            pltpu.VMEM((N_DP, 8, T), F32),
            pltpu.VMEM((8, D), F32),
            pltpu.VMEM((SIDE, 8, D), F32),
            pltpu.VMEM((8, D), F32),
            pltpu.VMEM((SIDE, 8, D), F32),
            pltpu.VMEM((H, D, T), BF16),
            pltpu.VMEM((H, T, T), F32),
            pltpu.VMEM((H, T, T), BF16),
            pltpu.VMEM((H, T, D), F32),
            pltpu.VMEM((H, T, D), BF16),
            pltpu.VMEM((H, T, D), F32),
            pltpu.VMEM((H, T, D), F32),
            pltpu.SemaphoreType.DMA((8,)),
            pltpu.SemaphoreType.DMA((8,)),
        ],
        compiler_params=pltpu.CompilerParams(
            collective_id=0, has_side_effects=True, vmem_limit_bytes=32 * 2**20
        ),
    )(queries, keys, values, output_gradient, log_decay, gain.reshape(1, H * D))
    return dq, dk, dv, dg.reshape(H * D)


def solution(mesh):
    return jax.shard_map(
        on_device,
        mesh=mesh,
        in_specs=(
            P("seq", "dp"),
            P("seq", "dp"),
            P("seq", "dp"),
            P("seq", "dp"),
            P("dp", "seq"),
            P("dp"),
        ),
        out_specs=(P("seq", "dp"), P("seq", "dp"), P("seq", "dp"), P("dp")),
        check_vma=False,
    )
```

```python
import functools

import jax
import jax.numpy as jnp
from jax import lax
from jax.experimental import pallas as pl
from jax.experimental.pallas import tpu as pltpu
from jax.sharding import PartitionSpec as P

MESH = pl.DeviceIdType.MESH
EPS = 1e-05
F32, BF16 = jnp.float32, jnp.bfloat16
HIGHEST = lax.Precision.HIGHEST
H, D, T = 4, 128, 128
SIDE, N_SEQ, N_DP = 8, 64, 16


def _ring(step):
    return min(step, SIDE - step)


STEPS = sorted(
    ((dy, dz) for dy in range(SIDE) for dz in range(SIDE) if dy or dz),
    key=lambda s: -(_ring(s[0]) + _ring(s[1])),
)
DP_STEPS = sorted(range(1, N_DP), key=lambda s: -_ring(s // 2))


def dot(a, b, ca=1, cb=0, precision=None):
    return lax.dot_general(
        a, b, (((ca,), (cb,)), ((), ())), precision=precision, preferred_element_type=F32
    )


def split(x):
    hi = x.astype(BF16)
    return hi, (x - hi.astype(F32)).astype(BF16)


def split_wide(x):
    return jnp.concatenate(split(x), axis=1)


def twice(x, axis):
    return jnp.concatenate([x, x], axis=axis)


def dot_fine_left(a, b):
    return dot(split_wide(a), twice(b, 0))


def dot_fine_right(a, b):
    return dot(twice(a, 1), jnp.concatenate(split(b), axis=0))


def dot_fine_right_t(a, b):
    return dot(twice(a, 1), split_wide(b), 1, 1)


def kernel(
    q_hbm, k_hbm, v_hbm, g_hbm, ld_hbm, gain_hbm,
    dq_ref, k_ref, v_ref, kg, vg, tail_ref, lat, dg_ref,
    q_ref, g_ref, ld_ref, gain_ref,
    snd1, rcv1, out1, inc, snd2, rcv2, out2, dec_snd, dec,
    stat_snd, stat, gz_snd, gz, gy_snd, gy,
    qt, weights, mixed, attn, d_attn,
    send_sems, recv_sems, load_sems,
):
    loads = [
        pltpu.make_async_copy(src, dst, load_sems.at[i])
        for i, (src, dst) in enumerate((
            (ld_hbm, ld_ref), (k_hbm, k_ref), (v_hbm, v_ref),
            (q_hbm, q_ref), (g_hbm, g_ref), (gain_hbm, gain_ref),
        ))
    ]
    for load in loads:
        load.start()
    me = lax.axis_index("seq")
    mine = lax.axis_index("dp")
    y, z = lax.div(me, SIDE), lax.rem(me, SIDE)
    rows = [lax.rem(y + k, SIDE) * SIDE for k in range(SIDE)]
    cols = [lax.rem(z + k, SIDE) for k in range(SIDE)]
    peers = [rows[dy] + cols[dz] for dy, dz in STEPS]
    partners = [lax.rem(mine + k, N_DP) for k in DP_STEPS]

    barrier = pltpu.get_barrier_semaphore()
    for p in peers:
        pl.semaphore_signal(barrier, inc=1, device_id={"seq": p}, device_id_type=MESH)
    for p in partners:
        pl.semaphore_signal(barrier, inc=1, device_id={"dp": p}, device_id_type=MESH)

    def send(src, dst, at, where):
        pltpu.make_async_remote_copy(
            src_ref=src, dst_ref=dst, send_sem=send_sems.at[at], recv_sem=recv_sems.at[at],
            device_id=where, device_id_type=MESH,
        ).start()

    def arrived(buffer, count, at, sems=recv_sems):
        part = buffer.at[pl.ds(0, count)]
        pltpu.make_async_copy(part, part, sems.at[at]).wait()

    def exchange(src, dst, at):
        for p in peers:
            send(src.at[p], dst.at[me], at, {"seq": p})
        dst[me] = src[me]

    row_i = lax.broadcasted_iota(jnp.int32, (T, T), 0)
    col_i = lax.broadcasted_iota(jnp.int32, (T, T), 1)
    lower = row_i >= col_i
    loads[0].wait()
    log_decay = ld_ref[...]
    cum_row = dot(log_decay, jnp.where(row_i <= col_i, 1.0, 0.0), precision=HIGHEST)
    cum_col = dot(jnp.where(lower, 1.0, 0.0), log_decay, 1, 1, precision=HIGHEST)
    last_row = cum_row[:, T - 1:]
    tail_row = jnp.exp(last_row - cum_row)
    lead_row = jnp.exp(cum_row)
    tail_col = jnp.exp(cum_col[T - 1:, :] - cum_col)
    lead_col = jnp.exp(cum_col)
    total = jnp.broadcast_to(jnp.exp(last_row), (H, T))

    def head(ref, h):
        return ref[:, h * D:(h + 1) * D]

    kt = []
    loads[1].wait()
    loads[2].wait()
    for h in range(H):
        dec_snd[h] = total[h:h + 1, :]
        kt.append(jnp.transpose(head(k_ref, h)))
        weighted = kt[h].astype(F32) * tail_row[h:h + 1, :]
        local = dot_fine_left(weighted, head(v_ref, h))
        snd1[pl.ds(16 * h, 16)] = local.reshape(16, 8, D)

    pl.semaphore_wait(barrier, N_SEQ - 1 + N_DP - 1)
    for p in peers:
        send(dec_snd.at[lax.div(p, 16)], dec.at[me], 1, {"seq": p})
    dec[me] = dec_snd[lax.div(me, 16)]
    exchange(snd1, rcv1, 0)

    for load in loads[3:]:
        load.wait()
    tail_ref[...] = tail_col
    for h in range(H):
        qh = head(q_ref, h)
        qt[h] = split_wide(jnp.transpose(qh).astype(F32) * lead_row[h:h + 1, :])
        w = jnp.where(
            lower,
            jnp.exp(jnp.minimum(cum_col[:, h:h + 1] - cum_row[h:h + 1, :], 0.0)),
            0.0,
        )
        weights[h] = w
        m = (dot(qh, kt[h]) * w).astype(BF16)
        mixed[h] = m
        attn[h] = dot(m, head(v_ref, h))

    arrived(dec, N_SEQ - 1, 1)
    arrived(rcv1, N_SEQ - 1, 0)
    state = jnp.zeros((8, D), F32)
    for c in range(N_SEQ):
        out1[c] = state
        state = dec[c] * state + rcv1[c]
    exchange(out1, inc, 2)
    arrived(inc, N_SEQ - 1, 2)

    def state_of(buffer, h):
        return buffer[pl.ds(16 * h, 16)].reshape(D, D)

    square = jnp.zeros((T, D), F32)
    cross = jnp.zeros((T, D), F32)
    for h in range(H):
        outer = dot_fine_right(head(q_ref, h), state_of(inc, h)) * lead_col[:, h:h + 1]
        a = attn[h] + outer
        attn[h] = a
        scaled = head(g_ref, h).astype(F32) * gain_ref[:, h * D:(h + 1) * D]
        square = square + a * a
        cross = cross + scaled * a
    square = jnp.sum(square, axis=1, keepdims=True)
    cross = jnp.sum(cross, axis=1, keepdims=True)
    both = jnp.where(col_i == 0, square, jnp.where(col_i == 1, cross, 0.0))
    stat_snd[...] = jnp.transpose(both)[0:8, :]
    for p in partners:
        send(stat_snd, stat.at[mine], 3, {"dp": p})
    stat[mine] = stat_snd[...]
    arrived(stat, N_DP - 1, 3)
    sums = stat[0]
    for c in range(1, N_DP):
        sums = sums + stat[c]
    sums = jnp.transpose(jnp.concatenate([sums] * 16, axis=0)) * (1.0 / (N_DP * H * D))
    gz_snd[...] = jnp.zeros_like(gz_snd)
    inv = lax.rsqrt(sums[:, 0:1] + EPS)
    cross_mean = inv * sums[:, 1:2]

    for h in range(H):
        g = head(g_ref, h).astype(F32)
        scaled = g * gain_ref[:, h * D:(h + 1) * D]
        normed = attn[h] * inv
        d = (inv * (scaled - normed * cross_mean)).astype(BF16)
        d_attn[h] = d
        snd2[pl.ds(16 * h, 16)] = dot(qt[h], twice(d, 0)).reshape(16, 8, D)
    exchange(snd2, rcv2, 4)
    for h in range(H):
        normed = attn[h] * inv
        gz_snd[h:h + 1, :] = jnp.sum(head(g_ref, h).astype(F32) * normed, axis=0, keepdims=True)
    for k in range(1, SIDE):
        send(gz_snd, gz.at[z], 5, {"seq": rows[0] + cols[k]})
    gz[z] = gz_snd[...]

    for h in range(H):
        qh, kh, vh, d = head(q_ref, h), head(k_ref, h), head(v_ref, h), d_attn[h]
        graded = (dot(d, vh, 1, 1) * weights[h]).astype(BF16)
        far = dot_fine_right_t(d, state_of(inc, h)) * lead_col[:, h:h + 1]
        dq_ref[:, h * D:(h + 1) * D] = (dot(graded, kh) + far).astype(BF16)
        kg[h] = dot(graded, qh, 0, 0)
        vg[h] = dot(mixed[h], d, 0, 0)

    arrived(rcv2, N_SEQ - 1, 4)
    state = jnp.zeros((8, D), F32)
    for c in reversed(range(N_SEQ)):
        out2[c] = state
        state = dec[c] * state + rcv2[c]
    exchange(out2, lat, 6)
    arrived(gz, SIDE - 1, 5)
    part = gz[0]
    for c in range(1, SIDE):
        part = part + gz[c]
    gy_snd[...] = part
    for k in range(1, SIDE):
        send(gy_snd, gy.at[y], 7, {"seq": rows[k] + cols[0]})
    gy[y] = gy_snd[...]

    arrived(gy, SIDE - 1, 7)
    part = gy[0]
    for c in range(1, SIDE):
        part = part + gy[c]
    dg_ref[...] = part[0:H, :]
    arrived(lat, N_SEQ - 1, 6)

    for buffer, count, at in (
        (rcv1, N_SEQ - 1, 0), (dec, N_SEQ - 1, 1), (inc, N_SEQ - 1, 2), (stat, N_DP - 1, 3),
        (rcv2, N_SEQ - 1, 4), (gz, SIDE - 1, 5), (lat, N_SEQ - 1, 6), (gy, SIDE - 1, 7),
    ):
        arrived(buffer, count, at, send_sems)


def finish(
    dq_ref, k_ref, v_ref, kg, vg, tail_ref, lat, dg_ref,
    dq_out, dk_out, dv_out, dg_out, dk_ref, dv_ref, sems,
):
    def start(src, dst, at):
        copy = pltpu.make_async_copy(src, dst, sems.at[at])
        copy.start()
        return copy

    copies = [start(dq_ref, dq_out, 0), start(dg_ref, dg_out, 1)]
    for h in range(H):
        part = pl.ds(h * D, D)
        late = lat[pl.ds(16 * h, 16)].reshape(D, D)
        far = dot_fine_right_t(v_ref[:, part], late)
        dk_ref[:, part] = (kg[h] + far * tail_ref[:, h:h + 1]).astype(BF16)
    copies.append(start(dk_ref, dk_out, 2))
    for h in range(H):
        part = pl.ds(h * D, D)
        late = lat[pl.ds(16 * h, 16)].reshape(D, D)
        far = dot_fine_right(k_ref[:, part], late)
        dv_ref[:, part] = (vg[h] + far * tail_ref[:, h:h + 1]).astype(BF16)
    copies.append(start(dv_ref, dv_out, 3))
    for copy in copies:
        copy.wait()


def on_device(queries, keys, values, output_gradient, log_decay, gain):
    vmem = pl.BlockSpec(memory_space=pltpu.VMEM)
    hbm = pl.BlockSpec(memory_space=pltpu.HBM)
    flat = (T, H * D)
    wide = jax.ShapeDtypeStruct(flat, BF16)
    small = jax.ShapeDtypeStruct((H, D), F32)
    tiles = pltpu.VMEM((N_SEQ, 8, D), F32)
    inside = [
        pltpu.VMEM(s, t)
        for s, t in (
            (flat, BF16), (flat, BF16), (flat, BF16), ((H, T, D), F32), ((H, T, D), F32),
            ((T, H), F32), ((N_SEQ, 8, D), F32), ((H, D), F32),
        )
    ]
    inputs = [
        pltpu.with_memory_space_constraint(x, pltpu.HBM)
        for x in (queries, keys, values, output_gradient, log_decay, gain.reshape(1, H * D))
    ]
    middle = pl.pallas_call(
        kernel,
        out_shape=inside,
        in_specs=[hbm] * 6,
        out_specs=(vmem,) * 8,
        scratch_shapes=[
            pltpu.VMEM(flat, BF16),
            pltpu.VMEM(flat, BF16),
            pltpu.VMEM((H, T), F32),
            pltpu.VMEM((1, H * D), F32),
            tiles, tiles, tiles, tiles, tiles, tiles, tiles,
            pltpu.VMEM((H, 1, D), F32),
            pltpu.VMEM((N_SEQ, 1, D), F32),
            pltpu.VMEM((8, T), F32),
            pltpu.VMEM((N_DP, 8, T), F32),
            pltpu.VMEM((8, D), F32),
            pltpu.VMEM((SIDE, 8, D), F32),
            pltpu.VMEM((8, D), F32),
            pltpu.VMEM((SIDE, 8, D), F32),
            pltpu.VMEM((H, D, 2 * T), BF16),
            pltpu.VMEM((H, T, T), F32),
            pltpu.VMEM((H, T, T), BF16),
            pltpu.VMEM((H, T, D), F32),
            pltpu.VMEM((H, T, D), BF16),
            pltpu.SemaphoreType.DMA((8,)),
            pltpu.SemaphoreType.DMA((8,)),
            pltpu.SemaphoreType.DMA((6,)),
        ],
        compiler_params=pltpu.CompilerParams(
            collective_id=0, has_side_effects=True, vmem_limit_bytes=32 * 2**20
        ),
    )(*inputs)
    middle = [pltpu.with_memory_space_constraint(x, pltpu.VMEM) for x in middle]
    dq, dk, dv, dg = pl.pallas_call(
        finish,
        out_shape=(wide, wide, wide, small),
        in_specs=[vmem] * 8,
        out_specs=(hbm,) * 4,
        scratch_shapes=[
            pltpu.VMEM(flat, BF16),
            pltpu.VMEM(flat, BF16),
            pltpu.SemaphoreType.DMA((4,)),
        ],
        compiler_params=pltpu.CompilerParams(vmem_limit_bytes=16 * 2**20),
    )(*middle)
    return dq, dk, dv, dg.reshape(H * D)


def solution(mesh):
    return jax.shard_map(
        on_device,
        mesh=mesh,
        in_specs=(
            P("seq", "dp"),
            P("seq", "dp"),
            P("seq", "dp"),
            P("seq", "dp"),
            P("dp", "seq"),
            P("dp"),
        ),
        out_specs=(P("seq", "dp"), P("seq", "dp"), P("seq", "dp"), P("dp")),
        check_vma=False,
    )
```
